32 devices in a mesh: nodes: 8 (over z, x), grid: 4 (over y, core).
Axes of the slice: x: 2, y: 2, z: 4, core: 2. Of those that a mesh axis runs over, the one named last changes fastest.
Arguments:
- block: float32 [256, 65536], P('grid', 'nodes')
- inv_sqrt_mass: float32 [65536], P('nodes'), may hold values from 0.6 to 1.6
- potential: float32 [65536], P('nodes'), may hold values from -2 to 1
- elem_scale: float32 [1024], P('nodes'), may hold values from 0.5 to 2
- connectivity: int32 [1024, 125], P('nodes'), may hold values from 0 to 10239, as said below
- elem_matrix: float32 [125, 125], replicated, as said below
Outputs:
- filtered_cyclic: float32 [256, 65536], P('grid', 'nodes')
- intersection: float32 [256, 256], P(None, 'grid')
The draws below stay inside these ranges and needn't reach their ends.
Inputs may be any that keep to these rules, and one draw needn't show every extreme that they name: `connectivity`: each row is an element of partition p = row // 128; its entries number the partition's 8192 own nodes from 0, then from 8192 the first 2048 nodes of the next partition. Element j of a partition uses nodes j * 64 to j * 64 + 2111; entries may repeat within an element. `elem_matrix`: Symmetric, with diagonal entries about 3 plus a full off-diagonal part.
All inputs are finite; a program needn't handle non-finite values.
Results may differ from the reference program's by a relative error of at most 0.0003.
Values sent between devices are 32-bit elements; how exact they have to be, the bound alone decides.
A program may use at most 64 MiB of HBM per device.

```python
import math
import jax
import jax.numpy as jnp
from jax import lax

BLOCK = 256
NPE = 125
ND = 8192
NODE_STRIDE = 64
RIM = 2048
NB = 128
SB = 16
E_DEV = 128
NODES = 65536
ELEMS = 1024
N_NODES = 8
N_GRID = 4


def draw_block(key, part):
    position = jnp.arange(NODES).astype(jnp.float32)
    rising = 1.0 + 2.0 * position / (NODES - 1)
    mix_key = jax.random.fold_in(key, 11)
    field_key = jax.random.fold_in(key, 23)
    noise_key = jax.random.fold_in(key, 37)
    mixing = jax.random.normal(mix_key, (BLOCK, 8), jnp.float32) * 8.0 ** (-0.5)
    fields = jax.random.normal(field_key, (8, NODES), jnp.float32)
    noise = jax.random.normal(noise_key, (BLOCK, NODES), jnp.float32)
    values = 0.7 * noise
    for common in range(8):
        values = values + mixing[:, common:common + 1] * fields[common][None, :]
    return values * rising[None, :]


def draw_connectivity(key, part):
    window = NODE_STRIDE + RIM
    offsets = jax.random.randint(key, (ELEMS, NPE), 0, window)
    offsets = offsets.at[:, 0].set(0).at[:, NPE - 1].set(window - 1)
    element = jnp.arange(ELEMS) % E_DEV
    return (element[:, None] * NODE_STRIDE + offsets).astype(jnp.int32)


def draw_elem_matrix(key, part):
    noise = jax.random.normal(key, (NPE, NPE), jnp.float32)
    return 0.03 * (noise + noise.T) + 3.0 * jnp.eye(NPE, dtype=jnp.float32)


def block_levels(rng, dims, split, smallest, top_value):
    loudness = 1.0
    for axis_at, parts in split:
        steps = jax.random.uniform(jax.random.fold_in(jax.random.fold_in(rng, 6), axis_at), (parts,), jnp.float32, smallest / len(split), top_value / len(split))
        loudness = loudness * jnp.repeat(jnp.exp(steps), dims[axis_at] // parts).reshape((-1,) + (1,) * (len(dims) - 1 - axis_at))
    return loudness


def setup_inputs(seed: int = 0) -> dict:
    streams_of = jax.random.split(jax.random.key(seed), 7)
    block = draw_block(jax.random.fold_in(streams_of[6], 71), 0)
    inv_sqrt_mass = jnp.clip(jnp.exp(math.log(1.6) - 0.98082923 * jax.random.uniform(streams_of[1], (NODES,), jnp.float32) ** block_levels(streams_of[1], (NODES,), ((0, 8),), -0.2, 0.2)), 0.6, 1.6)
    potential = jnp.clip(-2.0 + 3.0 * jax.random.uniform(streams_of[2], (NODES,), jnp.float32) ** block_levels(streams_of[2], (NODES,), ((0, 8),), -0.2, 0.2), -2.0, 1.0)
    elem_scale = jnp.clip(jnp.exp(math.log(2.0) - 1.3862944 * jax.random.uniform(streams_of[3], (ELEMS,), jnp.float32) ** block_levels(streams_of[3], (ELEMS,), ((0, 8),), -0.2, 0.2)), 0.5, 2.0)
    connectivity = draw_connectivity(jax.random.fold_in(streams_of[6], 71), 0)
    elem_matrix = draw_elem_matrix(jax.random.fold_in(streams_of[6], 71), 0)
    return dict(block=block, inv_sqrt_mass=inv_sqrt_mass, potential=potential, elem_scale=elem_scale, connectivity=connectivity, elem_matrix=elem_matrix)


def apply_operator(field, inv_sqrt_mass, potential, scale_parts, conn_parts, elem_matrix):
    scaled = inv_sqrt_mass[None, :] * field
    wide = jnp.concatenate([scaled, jnp.zeros((BLOCK, RIM), jnp.float32)], axis=1)
    starts = (jnp.arange(N_NODES) * ND).astype(jnp.int32)

    def add_part(total, item):
        part_conn, part_scale, start = item
        global_nodes = (part_conn.T + start).astype(jnp.int32)
        picked = wide[:, global_nodes]
        local = jnp.einsum('ab,sbe->sae', elem_matrix, picked, precision=lax.Precision.HIGHEST)
        local = local * part_scale[None, None, :]
        return (total.at[:, global_nodes].add(local), None)
    summed, unused = lax.scan(add_part, jnp.zeros((BLOCK, NODES + RIM), jnp.float32), (conn_parts, scale_parts, starts))
    return inv_sqrt_mass[None, :] * summed[:, :NODES] + potential[None, :] * field

def reference(block, inv_sqrt_mass, potential, elem_scale, connectivity, elem_matrix):
    conn_parts = connectivity.reshape(N_NODES, E_DEV, NPE)
    scale_parts = elem_scale.reshape(N_NODES, E_DEV)
    lowest, cut, top = (-2.0, 4.0, 32.0)
    half = (top - cut) / 2.0
    centre = (top + cut) / 2.0
    sigma = half / (lowest - centre)
    sigma_two = 1.0 / (2.0 / sigma - sigma)
    image = apply_operator(block, inv_sqrt_mass, potential, scale_parts, conn_parts, elem_matrix)
    first = sigma / half * (image - centre * block)
    image_two = apply_operator(first, inv_sqrt_mass, potential, scale_parts, conn_parts, elem_matrix)
    filtered = 2.0 * (sigma_two / half) * (image_two - centre * first) - sigma * sigma_two * block
    blocks = NODES // (N_NODES * NB)
    shaped = filtered.reshape(N_GRID, N_GRID, SB, blocks, N_NODES, NB)
    cyclic = shaped.transpose(1, 0, 2, 4, 3, 5).reshape(BLOCK, NODES)
    intersection = jnp.dot(cyclic, cyclic.T, precision=lax.Precision.HIGHEST) / NODES
    return (cyclic, intersection)
```

```python
import functools
import jax
import jax.numpy as jnp
from jax import lax
from jax.experimental import pallas as pl
from jax.experimental.pallas import tpu as pltpu
from jax.sharding import PartitionSpec as P

RIM = 2048
NB = 128
SB = 16
GROUP = 4
CHAINS = 4
BOTH = ("nodes", "grid")


def split(value):
    high = value.astype(jnp.bfloat16)
    return high, (value - high.astype(jnp.float32)).astype(jnp.bfloat16)


def dot(a, b):
    return jnp.dot(a, b, preferred_element_type=jnp.float32)


def operator_kernel(npe, index_ref, scale_ref, matrix_ref, wide_ref, out_ref, picked, local, *sums):
    groups = scale_ref.shape[0] // GROUP
    m_high, m_low = split(matrix_ref[...])
    picked[...] = jnp.zeros_like(picked)
    for total in sums:
        total[...] = jnp.zeros_like(total)

    def gather(first, i, m):
        node = index_ref[(first + m) * npe + i]
        picked[i : i + 1, m * 128 : (m + 1) * 128] = wide_ref[pl.ds(node, 1), :]

    for i in range(npe):
        for m in range(GROUP):
            gather(0, i, m)

    @pl.loop(0, groups)
    def _(g):
        here = g * GROUP
        later = jnp.minimum(g + 1, groups - 1) * GROUP
        high, low = split(picked[...])
        product = dot(m_high, high) + (dot(m_high, low) + dot(m_low, high))
        for m in range(GROUP):
            local[:, m * 128 : (m + 1) * 128] = (
                product[:, m * 128 : (m + 1) * 128] * scale_ref[here + m]
            )
        for i in range(npe):
            for m in range(GROUP):
                total = sums[(i * GROUP + m) % len(sums)]
                node = index_ref[(here + m) * npe + i]
                total[pl.ds(node, 1), :] += local[i : i + 1, m * 128 : (m + 1) * 128]
                gather(later, i, m)

    value = sums[0][...]
    for total in sums[1:]:
        value = value + total[...]
    out_ref[...] = value


def element_sums(wide, index, scale, matrix):
    count, npe = index.shape
    vmem = pl.BlockSpec(memory_space=pltpu.VMEM)
    smem = pl.BlockSpec(memory_space=pltpu.SMEM)
    rows = matrix.shape[0]
    return pl.pallas_call(
        functools.partial(operator_kernel, npe),
        out_shape=jax.ShapeDtypeStruct(wide.shape, jnp.float32),
        in_specs=[smem, smem, vmem, vmem],
        out_specs=vmem,
        scratch_shapes=[pltpu.VMEM((rows, GROUP * 128), jnp.float32)] * 2
        + [pltpu.VMEM(wide.shape, jnp.float32)] * CHAINS,
        compiler_params=pltpu.CompilerParams(vmem_limit_bytes=44 * 1024 * 1024),
    )(index.reshape(-1), scale, matrix, wide)


def shards(block, inv_sqrt_mass, potential, elem_scale, connectivity, elem_matrix):
    lowest, cut, top = (-2.0, 4.0, 32.0)
    half = (top - cut) / 2.0
    centre = (top + cut) / 2.0
    sigma = half / (lowest - centre)
    sigma_two = 1.0 / (2.0 / sigma - sigma)
    parts = lax.axis_size("nodes")
    columns = lax.axis_size("grid")
    states, owned = block.shape
    mine = owned // 2
    core = lax.axis_index("grid") % 2
    elements = connectivity.shape[0] // 2

    ups, downs = [], []
    for y in range(columns // 2):
        for t in range(2 * parts - 1):
            a = (t // 2) * columns + 2 * y + t % 2
            b = ((t + 1) // 2) * columns + 2 * y + (t + 1) % 2
            ups.append((a, b))
            downs.append((b, a))

    index = lax.dynamic_slice_in_dim(connectivity, core * elements, elements, 0) - core * mine
    scale = lax.dynamic_slice_in_dim(elem_scale, core * elements, elements, 0)
    mass = lax.dynamic_slice_in_dim(inv_sqrt_mass, core * mine, mine, 0)[:, None]
    pot = lax.dynamic_slice_in_dim(potential, core * mine, mine, 0)[:, None]
    pad = -elem_matrix.shape[0] % 128
    matrix = jnp.pad(elem_matrix, ((0, pad), (0, pad)))

    away = lax.dynamic_slice_in_dim(block, (1 - core) * mine, mine, 1)
    kept = lax.dynamic_slice_in_dim(block, core * mine, mine, 1)
    came = lax.ppermute(away, "grid", [(g, g ^ 1) for g in range(columns)])
    field = jnp.where(
        core == 0,
        jnp.concatenate([kept, came], axis=0),
        jnp.concatenate([came, kept], axis=0),
    ).T

    def operator(field):
        scaled = mass * field
        upper = lax.ppermute(scaled[:RIM], BOTH, downs)
        summed = element_sums(jnp.concatenate([scaled, upper], axis=0), index, scale, matrix)
        lower = lax.ppermute(summed[mine:], BOTH, ups)
        assembled = jnp.concatenate([summed[:RIM] + lower, summed[RIM:mine]], axis=0)
        return mass * assembled + pot * field

    first = sigma / half * (operator(field) - centre * field)
    filtered = 2.0 * (sigma_two / half) * (operator(first) - centre * first) - sigma * sigma_two * field
    wide = filtered.T

    blocks = mine // (parts * NB)
    shaped = wide.reshape(2, columns, SB, blocks, parts, NB).transpose(4, 1, 0, 2, 3, 5)
    shaped = shaped.reshape(parts * columns, 2 * SB, blocks * NB)
    moved = lax.all_to_all(shaped, BOTH, split_axis=0, concat_axis=0, tiled=True)
    cyclic = (
        moved.reshape(parts, columns // 2, 2, 2 * SB, blocks * NB)
        .transpose(1, 3, 0, 2, 4)
        .reshape(states, owned)
    )

    y = lax.axis_index("grid") // 2
    quarter = mine // 2
    over = lax.dynamic_slice_in_dim(wide, (1 - y) * quarter, quarter, 1)
    stay = lax.dynamic_slice_in_dim(wide, y * quarter, quarter, 1)
    other = lax.ppermute(over, "grid", [(g, g ^ 2) for g in range(columns)])
    whole = jnp.where(
        y == 0, jnp.concatenate([stay, other], axis=0), jnp.concatenate([other, stay], axis=0)
    )
    gram = jnp.dot(whole, whole.T, precision=lax.Precision.HIGHEST) * (1.0 / (owned * parts))
    gram = lax.psum(gram, BOTH)
    count = columns * states
    gram = gram.reshape(columns, columns, SB, columns, columns, SB)
    gram = gram.transpose(1, 0, 2, 4, 3, 5).reshape(count, count)
    panel = lax.dynamic_slice_in_dim(gram, lax.axis_index("grid") * states, states, 1)
    return cyclic, panel


def solution(mesh):
    placed = (P("grid", "nodes"), P("nodes"), P("nodes"), P("nodes"), P("nodes", None), P())
    return jax.shard_map(
        shards,
        mesh=mesh,
        in_specs=placed,
        out_specs=(P("grid", "nodes"), P(None, "grid")),
        check_vma=False,
    )
```

```python
import functools
import jax
import jax.numpy as jnp
from jax import lax
from jax.experimental import pallas as pl
from jax.experimental.pallas import tpu as pltpu
from jax.sharding import PartitionSpec as P

RIM = 2048
NB = 128
SB = 16
GROUP = 4
CHAINS = 4
BOTH = ("nodes", "grid")


def split(value):
    high = value.astype(jnp.bfloat16)
    return high, (value - high.astype(jnp.float32)).astype(jnp.bfloat16)


def dot(a, b):
    return jnp.dot(a, b, preferred_element_type=jnp.float32)


def operator_kernel(npe, index_ref, scale_ref, matrix_ref, wide_ref, out_ref, picked, local, *sums):
    groups = scale_ref.shape[0] // GROUP
    m_high, m_low = split(matrix_ref[...])
    picked[...] = jnp.zeros_like(picked)
    for total in sums:
        total[...] = jnp.zeros_like(total)

    def gather(first, i, m):
        node = index_ref[(first + m) * npe + i]
        picked[i : i + 1, m * 128 : (m + 1) * 128] = wide_ref[pl.ds(node, 1), :]

    for i in range(npe):
        for m in range(GROUP):
            gather(0, i, m)

    @pl.loop(0, groups)
    def _(g):
        here = g * GROUP
        later = jnp.minimum(g + 1, groups - 1) * GROUP
        high, low = split(picked[...])
        product = dot(m_high, high) + (dot(m_high, low) + dot(m_low, high))
        for m in range(GROUP):
            local[:, m * 128 : (m + 1) * 128] = (
                product[:, m * 128 : (m + 1) * 128] * scale_ref[here + m]
            )
        for i in range(npe):
            for m in range(GROUP):
                total = sums[(i * GROUP + m) % len(sums)]
                node = index_ref[(here + m) * npe + i]
                total[pl.ds(node, 1), :] += local[i : i + 1, m * 128 : (m + 1) * 128]
                gather(later, i, m)

    value = sums[0][...]
    for total in sums[1:]:
        value = value + total[...]
    out_ref[...] = value


def element_sums(wide, index, scale, matrix):
    count, npe = index.shape
    vmem = pl.BlockSpec(memory_space=pltpu.VMEM)
    smem = pl.BlockSpec(memory_space=pltpu.SMEM)
    rows = matrix.shape[0]
    return pl.pallas_call(
        functools.partial(operator_kernel, npe),
        out_shape=jax.ShapeDtypeStruct(wide.shape, jnp.float32),
        in_specs=[smem, smem, vmem, vmem],
        out_specs=vmem,
        scratch_shapes=[pltpu.VMEM((rows, GROUP * 128), jnp.float32)] * 2
        + [pltpu.VMEM(wide.shape, jnp.float32)] * CHAINS,
        compiler_params=pltpu.CompilerParams(vmem_limit_bytes=44 * 1024 * 1024),
    )(index.reshape(-1), scale, matrix, wide)


STRIDE = 11
MESH = pl.DeviceIdType.MESH


def others(count, me, body):
    stride = STRIDE if count % STRIDE else 1

    def step(s, carry):
        body(lax.rem(me + s * stride, count))
        return carry

    lax.fori_loop(1, count, step, 0)


def greet(devices):
    barrier = pltpu.get_barrier_semaphore()
    for device in devices:
        pl.semaphore_signal(barrier, inc=1, device_id=device, device_id_type=MESH)
    pl.semaphore_wait(barrier, len(devices))


def finish_kernel(
    parts, columns, pieces, weight,
    sums_ref, one_ref, two_ref, coef_ref, out_ref, panel_ref,
    flat, send, rim, raw, high, low, gram, collected, stage, panel,
    rim_sem, swap_sem, move_send, move_recv, part_send, part_recv, row_send, row_recv, own_sem,
):
    p, g = lax.axis_index("nodes"), lax.axis_index("grid")
    y, k = g // 2, lax.rem(g, 2)
    count = parts * columns
    me = p * columns + g
    t, last = 2 * p + k, 2 * parts - 1
    mine = flat.shape[1]
    quarter = mine // 4
    width = mine // parts
    span = width // pieces
    states = panel_ref.shape[1]
    total_states = gram.shape[0]
    owners = total_states // 8

    def place(d):
        return (d // columns, lax.rem(d, columns))

    barrier = pltpu.get_barrier_semaphore()
    others(
        count, me,
        lambda d: pl.semaphore_signal(barrier, inc=1, device_id=place(d), device_id_type=MESH),
    )
    pl.semaphore_wait(barrier, count - 1)

    def rim_copy():
        up = t + 1
        return pltpu.make_async_remote_copy(
            src_ref=sums_ref.at[pl.ds(mine, RIM)], dst_ref=rim,
            send_sem=rim_sem.at[0], recv_sem=rim_sem.at[1],
            device_id=(up // 2, 2 * y + lax.rem(up, 2)), device_id_type=MESH,
        )

    @pl.when(t < last)
    def _():
        rim_copy().start()

    @pl.when(t == 0)
    def _():
        rim[...] = jnp.zeros_like(rim)

    def swap_copy(h):
        start = pl.multiple_of((2 * h + 1 - y) * quarter, 128)
        return pltpu.make_async_remote_copy(
            src_ref=flat.at[:, pl.ds(start, quarter)],
            dst_ref=raw.at[h, pl.ds(pl.multiple_of(y * 128, 128), 128)],
            send_sem=swap_sem.at[0, h], recv_sem=swap_sem.at[1, h],
            device_id=(p, 2 * (1 - y) + k), device_id_type=MESH,
        )

    def landing(d, h):
        dp, dg = place(d)
        row = pl.multiple_of((dg // 2) * 32, 32)
        column = pl.multiple_of((dp * 2 + lax.rem(dg, 2)) * width + h * span, 128)
        return out_ref.at[pl.ds(row, 32), pl.ds(column, span)]

    def move(d, h, source):
        return pltpu.make_async_remote_copy(
            src_ref=send.at[d, :, pl.ds(h * span, span)], dst_ref=landing(source, h),
            send_sem=move_send.at[h, d], recv_sem=move_recv.at[h, source],
            device_id=place(d), device_id_type=MESH,
        )

    def combine(b, with_rim):
        at = pl.multiple_of(b * 128, 128)
        rows = pl.ds(at, 128)
        value = sums_ref[rows, :]
        if with_rim:
            value = value + rim[rows, :]
        result = (
            value.T * coef_ref[2:3, rows]
            + two_ref[rows, :].T * coef_ref[3:4, rows]
            + one_ref[rows, :].T * coef_ref[4:5, rows]
        )
        flat[:, rows] = result
        l, q = b // parts, lax.rem(b, parts)
        for c in range(columns):
            for kk in range(2):
                send[q * columns + c, kk * SB : (kk + 1) * SB, pl.ds(pl.multiple_of(l * 128, 128), 128)] = (
                    result[kk * states + c * SB : kk * states + (c + 1) * SB, :]
                )

    half = mine // 256

    def keep(h):
        start = pl.multiple_of((2 * h + y) * quarter, 128)
        raw[h, pl.ds(pl.multiple_of(y * 128, 128), 128), :] = flat[:, pl.ds(start, quarter)]

    @pl.loop(half, 2 * half)
    def _(b):
        combine(b, False)

    swap_copy(1).start()
    if pieces == 2:
        others(count, me, lambda d: move(d, 1, me).start())
    keep(1)

    @pl.when(t > 0)
    def _():
        rim_copy().wait_recv()

    @pl.loop(0, half)
    def _(b):
        combine(b, True)

    swap_copy(0).start()
    others(count, me, lambda d: move(d, 0, me).start())
    keep(0)
    own = [
        pltpu.make_async_copy(send.at[me, :, pl.ds(h * span, span)], landing(me, h), own_sem.at[h])
        for h in range(pieces)
    ]
    for copy in own:
        copy.start()

    across = (((1,), (1,)), ((), ()))

    def product(a, b):
        return lax.dot_general(a, b, across, preferred_element_type=jnp.float32)

    for h in (1, 0):
        swap_copy(h).wait_recv()
        for c in range(columns):
            for kb in range(columns):
                upper, lower = split(raw[h, kb * states + c * SB : kb * states + (c + 1) * SB, :])
                to = c * states + kb * SB
                high[to : to + SB, :] = upper
                low[to : to + SB, :] = lower
        mixed = product(high[...], low[...])
        value = product(high[...], high[...]) + (mixed + mixed.T)
        if h == 1:
            gram[...] = value
        else:
            gram[...] = gram[...] + value

    def rows_of(d):
        return pl.ds(pl.multiple_of(d * 8, 8), 8)

    def part(d, source):
        return pltpu.make_async_remote_copy(
            src_ref=gram.at[rows_of(d)], dst_ref=collected.at[source],
            send_sem=part_send.at[d], recv_sem=part_recv.at[source],
            device_id=place(d), device_id_type=MESH,
        )

    def if_owner(d, body):
        if owners == count:
            body()
        else:
            pl.when(d < owners)(body)

    def row(d, source):
        return pltpu.make_async_remote_copy(
            src_ref=stage.at[lax.rem(d, columns)], dst_ref=panel.at[rows_of(source)],
            send_sem=row_send.at[d], recv_sem=row_recv.at[source],
            device_id=place(d), device_id_type=MESH,
        )

    others(count, me, lambda d: if_owner(d, lambda: part(d, me).start()))
    stage[...] = jnp.zeros_like(stage)

    def own_rows():
        collected[me] = gram[rows_of(me), :]
        others(count, me, lambda d: part(me, d).wait_recv())
        sums = lax.fori_loop(
            0, count, lambda d, value: value + collected[d], jnp.zeros(collected.shape[1:], jnp.float32)
        )
        sums = sums * weight
        for c in range(columns):
            stage[c, :, :states] = sums[:, c * states : (c + 1) * states]
        panel[rows_of(me), :] = stage[g]
        others(count, me, lambda d: row(d, me).start())

    if_owner(me, own_rows)
    others(count, me, lambda d: if_owner(d, lambda: row(me, d).wait_recv()))
    panel_ref[...] = panel[:, :states]

    for h in range(pieces):
        others(count, me, lambda d: move(me, h, d).wait_recv())
    for h in range(pieces):
        others(count, me, lambda d: move(d, h, me).wait_send())
    for copy in own:
        copy.wait()
    for h in (0, 1):
        swap_copy(h).wait_send()
    others(count, me, lambda d: if_owner(d, lambda: part(d, me).wait_send()))
    if_owner(me, lambda: others(count, me, lambda d: row(d, me).wait_send()))

    @pl.when(t < last)
    def _():
        rim_copy().wait_send()


def finish(parts, columns, states, owned, sums, one, two, coef):
    mine = owned // 2
    count = parts * columns
    width = mine // parts
    pieces = 2 if width % 256 == 0 else 1
    total = columns * states
    vmem = pl.BlockSpec(memory_space=pltpu.VMEM)
    dma = pltpu.SemaphoreType.DMA
    f32, bf16 = jnp.float32, jnp.bfloat16
    return pl.pallas_call(
        functools.partial(finish_kernel, parts, columns, pieces, 1.0 / (owned * parts)),
        out_shape=(
            jax.ShapeDtypeStruct((states, owned), f32),
            jax.ShapeDtypeStruct((total, states), f32),
        ),
        in_specs=[vmem] * 4,
        out_specs=(pl.BlockSpec(memory_space=pl.ANY), vmem),
        scratch_shapes=[
            pltpu.VMEM((2 * states, mine), f32),
            pltpu.VMEM((count, 2 * SB, width), f32),
            pltpu.VMEM((RIM, 2 * states), f32),
            pltpu.VMEM((2, total, mine // 4), f32),
            pltpu.VMEM((total, mine // 4), bf16),
            pltpu.VMEM((total, mine // 4), bf16),
            pltpu.VMEM((total, total), f32),
            pltpu.VMEM((count, 8, total), f32),
            pltpu.VMEM((columns, 8, 128), f32),
            pltpu.VMEM((total, 128), f32),
            dma((2,)), dma((2, 2)), dma((pieces, count)), dma((pieces, count)),
            dma((count,)), dma((count,)), dma((count,)), dma((count,)), dma((pieces,)),
        ],
        compiler_params=pltpu.CompilerParams(
            collective_id=0, has_side_effects=True, vmem_limit_bytes=44 * 1024 * 1024
        ),
    )(sums, one, two, coef)


def shards(block, inv_sqrt_mass, potential, elem_scale, connectivity, elem_matrix):
    lowest, cut, top = (-2.0, 4.0, 32.0)
    half = (top - cut) / 2.0
    centre = (top + cut) / 2.0
    sigma = half / (lowest - centre)
    sigma_two = 1.0 / (2.0 / sigma - sigma)
    alpha, beta, gamma = sigma / half, 2.0 * (sigma_two / half), sigma * sigma_two
    parts = lax.axis_size("nodes")
    columns = lax.axis_size("grid")
    states, owned = block.shape
    mine = owned // 2
    core = lax.axis_index("grid") % 2
    elements = connectivity.shape[0] // 2

    ups, downs = [], []
    for y in range(columns // 2):
        for t in range(2 * parts - 1):
            a = (t // 2) * columns + 2 * y + t % 2
            b = ((t + 1) // 2) * columns + 2 * y + (t + 1) % 2
            ups.append((a, b))
            downs.append((b, a))

    index = lax.dynamic_slice_in_dim(connectivity, core * elements, elements, 0) - core * mine
    scale = lax.dynamic_slice_in_dim(elem_scale, core * elements, elements, 0)
    pad = -elem_matrix.shape[0] % 128
    matrix = jnp.pad(elem_matrix, ((0, pad), (0, pad)))

    shift = potential - centre
    inverse = 1.0 / inv_sqrt_mass
    zero = jnp.zeros_like(shift)
    coef = jnp.stack(
        [
            alpha * inv_sqrt_mass * inv_sqrt_mass,
            alpha * shift,
            beta * inv_sqrt_mass,
            beta * shift * inverse,
            -gamma * inverse,
            zero,
            zero,
            zero,
        ]
    )
    coef = lax.dynamic_slice_in_dim(coef, core * mine, mine, 1)
    coef = jnp.concatenate([coef, lax.ppermute(coef[:, :RIM], BOTH, downs)], axis=1)

    scaled = inv_sqrt_mass[None, :] * block
    away = lax.dynamic_slice_in_dim(scaled, (1 - core) * mine, mine, 1)
    kept = lax.dynamic_slice_in_dim(scaled, core * mine, mine, 1)
    came = lax.ppermute(away, "grid", [(g, g ^ 1) for g in range(columns)])
    field = jnp.where(
        core == 0,
        jnp.concatenate([kept, came], axis=0),
        jnp.concatenate([came, kept], axis=0),
    ).T
    one = jnp.concatenate([field, lax.ppermute(field[:RIM], BOTH, downs)], axis=0)

    sums = element_sums(one, index, scale, matrix)
    lower = lax.ppermute(sums[mine:], BOTH, ups)
    upper = lax.ppermute(sums[:RIM], BOTH, downs)
    assembled = jnp.concatenate([sums[:RIM] + lower, sums[RIM:mine], sums[mine:] + upper], axis=0)
    two = coef[0][:, None] * assembled + coef[1][:, None] * one
    sums = element_sums(two, index, scale, matrix)
    return finish(parts, columns, states, owned, sums, one, two, coef)


def solution(mesh):
    placed = (P("grid", "nodes"), P("nodes"), P("nodes"), P("nodes"), P("nodes", None), P())
    return jax.shard_map(
        shards,
        mesh=mesh,
        in_specs=placed,
        out_specs=(P("grid", "nodes"), P(None, "grid")),
        check_vma=False,
    )
```

```python
import functools
import jax
import jax.numpy as jnp
from jax import lax
from jax.experimental import pallas as pl
from jax.experimental.pallas import tpu as pltpu
from jax.sharding import PartitionSpec as P

RIM = 2048
NB = 128
SB = 16
GROUP = 4
CHAINS = 8
BOTH = ("nodes", "grid")


def split(value):
    high = value.astype(jnp.bfloat16)
    return high, (value - high.astype(jnp.float32)).astype(jnp.bfloat16)


def dot(a, b):
    return jnp.dot(a, b, preferred_element_type=jnp.float32)


def operator_kernel(npe, index_ref, scale_ref, matrix_ref, wide_ref, out_ref, picked, local, *sums):
    groups = scale_ref.shape[0] // GROUP
    m_high, m_low = split(matrix_ref[...])
    picked[...] = jnp.zeros_like(picked)
    for total in sums:
        total[...] = jnp.zeros_like(total)

    def gather(first, i, m):
        node = index_ref[(first + m) * npe + i]
        picked[i : i + 1, m * 128 : (m + 1) * 128] = wide_ref[pl.ds(node, 1), :]

    for i in range(npe):
        for m in range(GROUP):
            gather(0, i, m)

    @pl.loop(0, groups)
    def _(g):
        here = g * GROUP
        later = jnp.minimum(g + 1, groups - 1) * GROUP
        high, low = split(picked[...])
        product = dot(m_high, high) + (dot(m_high, low) + dot(m_low, high))
        for m in range(GROUP):
            local[:, m * 128 : (m + 1) * 128] = (
                product[:, m * 128 : (m + 1) * 128] * scale_ref[here + m]
            )
        for i in range(npe):
            for m in range(GROUP):
                total = sums[(i * GROUP + m) % len(sums)]
                node = index_ref[(here + m) * npe + i]
                total[pl.ds(node, 1), :] += local[i : i + 1, m * 128 : (m + 1) * 128]
                gather(later, i, m)

    value = sums[0][...]
    for total in sums[1:]:
        value = value + total[...]
    out_ref[...] = value


def element_sums(wide, index, scale, matrix):
    count, npe = index.shape
    vmem = pl.BlockSpec(memory_space=pltpu.VMEM)
    smem = pl.BlockSpec(memory_space=pltpu.SMEM)
    rows = matrix.shape[0]
    return pl.pallas_call(
        functools.partial(operator_kernel, npe),
        out_shape=jax.ShapeDtypeStruct(wide.shape, jnp.float32),
        in_specs=[smem, smem, vmem, vmem],
        out_specs=vmem,
        scratch_shapes=[pltpu.VMEM((rows, GROUP * 128), jnp.float32)] * 2
        + [pltpu.VMEM(wide.shape, jnp.float32)] * CHAINS,
        compiler_params=pltpu.CompilerParams(vmem_limit_bytes=44 * 1024 * 1024),
    )(index.reshape(-1), scale, matrix, wide)


STRIDE = 11
MESH = pl.DeviceIdType.MESH


def others(count, me, body, begin=1, end=None):
    stride = STRIDE if count % STRIDE else 1

    def step(s, carry):
        body(lax.rem(me + s * stride, count))
        return carry

    lax.fori_loop(begin, end or count, step, 0)


def finish_kernel(
    parts, columns, pieces, weight,
    sums_ref, one_ref, two_ref, coef_ref, out_ref, panel_ref,
    flat, send, rim, raw, high, low, gram, collected, stage, panel,
    rim_sem, swap_sem, move_send, move_recv, part_send, part_recv, row_send, row_recv, own_sem,
):
    p, g = lax.axis_index("nodes"), lax.axis_index("grid")
    y, k = g // 2, lax.rem(g, 2)
    count = parts * columns
    me = p * columns + g
    t, last = 2 * p + k, 2 * parts - 1
    mine = flat.shape[1]
    quarter = mine // 4
    width = mine // parts
    span = width // pieces
    states = panel_ref.shape[1]
    total_states = gram.shape[0]
    owners = total_states // 8

    def place(d):
        return (d // columns, lax.rem(d, columns))

    barrier = pltpu.get_barrier_semaphore()
    others(
        count, me,
        lambda d: pl.semaphore_signal(barrier, inc=1, device_id=place(d), device_id_type=MESH),
    )
    pl.semaphore_wait(barrier, count - 1)

    def rim_copy():
        up = t + 1
        return pltpu.make_async_remote_copy(
            src_ref=sums_ref.at[pl.ds(mine, RIM)], dst_ref=rim,
            send_sem=rim_sem.at[0], recv_sem=rim_sem.at[1],
            device_id=(up // 2, 2 * y + lax.rem(up, 2)), device_id_type=MESH,
        )

    @pl.when(t < last)
    def _():
        rim_copy().start()

    @pl.when(t == 0)
    def _():
        rim[...] = jnp.zeros_like(rim)

    def swap_copy(h):
        start = pl.multiple_of((2 * h + 1 - y) * quarter, 128)
        return pltpu.make_async_remote_copy(
            src_ref=flat.at[:, pl.ds(start, quarter)],
            dst_ref=raw.at[h, pl.ds(pl.multiple_of(y * 128, 128), 128)],
            send_sem=swap_sem.at[0, h], recv_sem=swap_sem.at[1, h],
            device_id=(p, 2 * (1 - y) + k), device_id_type=MESH,
        )

    def landing(d, h):
        dp, dg = place(d)
        row = pl.multiple_of((dg // 2) * 32, 32)
        column = pl.multiple_of((dp * 2 + lax.rem(dg, 2)) * width + h * span, 128)
        return out_ref.at[pl.ds(row, 32), pl.ds(column, span)]

    def move(d, h, source):
        return pltpu.make_async_remote_copy(
            src_ref=send.at[d, :, pl.ds(h * span, span)], dst_ref=landing(source, h),
            send_sem=move_send.at[h, d], recv_sem=move_recv.at[h, source],
            device_id=place(d), device_id_type=MESH,
        )

    def combine(b, with_rim):
        at = pl.multiple_of(b * 128, 128)
        rows = pl.ds(at, 128)
        value = sums_ref[rows, :]
        if with_rim:
            value = value + rim[rows, :]
        result = (
            value.T * coef_ref[3:4, rows]
            + two_ref[rows, :].T * coef_ref[4:5, rows]
            + one_ref[rows, :].T * coef_ref[5:6, rows]
        )
        flat[:, rows] = result
        l, q = b // parts, lax.rem(b, parts)
        for c in range(columns):
            for kk in range(2):
                send[q * columns + c, kk * SB : (kk + 1) * SB, pl.ds(pl.multiple_of(l * 128, 128), 128)] = (
                    result[kk * states + c * SB : kk * states + (c + 1) * SB, :]
                )

    half = mine // 256

    def keep(h):
        start = pl.multiple_of((2 * h + y) * quarter, 128)
        raw[h, pl.ds(pl.multiple_of(y * 128, 128), 128), :] = flat[:, pl.ds(start, quarter)]

    @pl.loop(half, 2 * half)
    def _(b):
        combine(b, False)

    swap_copy(1).start()
    if pieces == 2:
        others(count, me, lambda d: move(d, 1, me).start())
    keep(1)

    @pl.when(t > 0)
    def _():
        rim_copy().wait_recv()

    @pl.loop(0, half)
    def _(b):
        combine(b, True)

    swap_copy(0).start()
    others(count, me, lambda d: move(d, 0, me).start(), 1, count // 2)
    keep(0)
    own = [
        pltpu.make_async_copy(send.at[me, :, pl.ds(h * span, span)], landing(me, h), own_sem.at[h])
        for h in range(pieces)
    ]
    for copy in own:
        copy.start()

    across = (((1,), (1,)), ((), ()))

    def product(a, b):
        return lax.dot_general(a, b, across, preferred_element_type=jnp.float32)

    for h in (1, 0):
        swap_copy(h).wait_recv()
        for c in range(columns):
            for kb in range(columns):
                upper, lower = split(raw[h, kb * states + c * SB : kb * states + (c + 1) * SB, :])
                to = c * states + kb * SB
                high[to : to + SB, :] = upper
                low[to : to + SB, :] = lower
        mixed = product(high[...], low[...])
        value = product(high[...], high[...]) + (mixed + mixed.T)
        if h == 1:
            gram[...] = value
        else:
            gram[...] = gram[...] + value

    def rows_of(d):
        return pl.ds(pl.multiple_of(d * 8, 8), 8)

    def part(d, source):
        return pltpu.make_async_remote_copy(
            src_ref=gram.at[rows_of(d)], dst_ref=collected.at[source],
            send_sem=part_send.at[d], recv_sem=part_recv.at[source],
            device_id=place(d), device_id_type=MESH,
        )

    def if_owner(d, body):
        if owners == count:
            body()
        else:
            pl.when(d < owners)(body)

    def row(d, source):
        return pltpu.make_async_remote_copy(
            src_ref=stage.at[lax.rem(d, columns)], dst_ref=panel.at[rows_of(source)],
            send_sem=row_send.at[d], recv_sem=row_recv.at[source],
            device_id=place(d), device_id_type=MESH,
        )

    others(count, me, lambda d: if_owner(d, lambda: part(d, me).start()))
    others(count, me, lambda d: move(d, 0, me).start(), count // 2, count)
    stage[...] = jnp.zeros_like(stage)

    def own_rows():
        collected[me] = gram[rows_of(me), :]
        others(count, me, lambda d: part(me, d).wait_recv())
        sums = lax.fori_loop(
            0, count, lambda d, value: value + collected[d], jnp.zeros(collected.shape[1:], jnp.float32)
        )
        sums = sums * weight
        for c in range(columns):
            stage[c, :, :states] = sums[:, c * states : (c + 1) * states]
        panel[rows_of(me), :] = stage[g]
        others(count, me, lambda d: row(d, me).start())

    if_owner(me, own_rows)
    others(count, me, lambda d: if_owner(d, lambda: row(me, d).wait_recv()))
    panel_ref[...] = panel[:, :states]

    for h in range(pieces):
        others(count, me, lambda d: move(me, h, d).wait_recv())
    for h in range(pieces):
        others(count, me, lambda d: move(d, h, me).wait_send())
    for copy in own:
        copy.wait()
    for h in (0, 1):
        swap_copy(h).wait_send()
    others(count, me, lambda d: if_owner(d, lambda: part(d, me).wait_send()))
    if_owner(me, lambda: others(count, me, lambda d: row(d, me).wait_send()))

    @pl.when(t < last)
    def _():
        rim_copy().wait_send()


def finish(parts, columns, states, owned, sums, one, two, coef):
    mine = owned // 2
    count = parts * columns
    width = mine // parts
    pieces = 2 if width % 256 == 0 else 1
    total = columns * states
    vmem = pl.BlockSpec(memory_space=pltpu.VMEM)
    dma = pltpu.SemaphoreType.DMA
    f32, bf16 = jnp.float32, jnp.bfloat16
    return pl.pallas_call(
        functools.partial(finish_kernel, parts, columns, pieces, 1.0 / (owned * parts)),
        out_shape=(
            jax.ShapeDtypeStruct((states, owned), f32),
            jax.ShapeDtypeStruct((total, states), f32),
        ),
        in_specs=[vmem] * 4,
        out_specs=(pl.BlockSpec(memory_space=pl.ANY), vmem),
        scratch_shapes=[
            pltpu.VMEM((2 * states, mine), f32),
            pltpu.VMEM((count, 2 * SB, width), f32),
            pltpu.VMEM((RIM, 2 * states), f32),
            pltpu.VMEM((2, total, mine // 4), f32),
            pltpu.VMEM((total, mine // 4), bf16),
            pltpu.VMEM((total, mine // 4), bf16),
            pltpu.VMEM((total, total), f32),
            pltpu.VMEM((count, 8, total), f32),
            pltpu.VMEM((columns, 8, 128), f32),
            pltpu.VMEM((total, 128), f32),
            dma((2,)), dma((2, 2)), dma((pieces, count)), dma((pieces, count)),
            dma((count,)), dma((count,)), dma((count,)), dma((count,)), dma((pieces,)),
        ],
        compiler_params=pltpu.CompilerParams(
            collective_id=0, has_side_effects=True, vmem_limit_bytes=44 * 1024 * 1024
        ),
    )(sums, one, two, coef)


def seat(columns):
    p, g = lax.axis_index("nodes"), lax.axis_index("grid")
    return p, g, g // 2, lax.rem(g, 2)


def remote(source, target, sems, slot, device):
    return pltpu.make_async_remote_copy(
        src_ref=source, dst_ref=target, send_sem=sems.at[0, slot], recv_sem=sems.at[1, slot],
        device_id=device, device_id_type=MESH,
    )


def spread_kernel(
    parts, columns, block_ref, coef_ref, one_ref, wide_ref, scaled, whole, tail, sems
):
    p, g, y, k = seat(columns)
    states, owned = block_ref.shape
    mine = owned // 2
    barrier = pltpu.get_barrier_semaphore()
    pl.semaphore_signal(barrier, inc=1, device_id=(p, 2 * y + 1 - k), device_id_type=MESH)

    @pl.when(p > 0)
    def _():
        pl.semaphore_signal(barrier, inc=1, device_id=(p - 1, 2 * y + 1), device_id_type=MESH)

    @pl.when((k == 1) & (p < parts - 1))
    def _():
        for kk in range(2):
            pl.semaphore_signal(barrier, inc=1, device_id=(p + 1, 2 * y + kk), device_id_type=MESH)

    rows = pl.ds(pl.multiple_of(k * states, 8), states)

    @pl.loop(0, owned // 512)
    def _(b):
        at = pl.ds(pl.multiple_of(b * 512, 128), 512)
        scaled[:, at] = block_ref[:, at] * coef_ref[0:1, at]

    before = jnp.where(p > 0, 1, 0)
    after = jnp.where((k == 1) & (p < parts - 1), 2, 0)
    pl.semaphore_wait(barrier, 1 + before + after)

    def back(r=rows, slot=0):
        return remote(scaled.at[:, pl.ds(0, RIM)], tail.at[r], sems, slot, (p - 1, 2 * y + 1))

    def back_coef():
        return remote(
            coef_ref.at[:, pl.ds(0, RIM)], wide_ref.at[:, pl.ds(mine, RIM)], sems, 2,
            (p - 1, 2 * y + 1),
        )

    def to_second():
        return remote(
            scaled.at[:, pl.ds(mine, mine)], whole.at[rows, pl.ds(0, mine)], sems, 3,
            (p, 2 * y + 1),
        )

    def to_first():
        return remote(
            scaled.at[:, pl.ds(0, mine + RIM)], whole.at[rows], sems, 4, (p, 2 * y)
        )

    first, second = k == 0, k == 1
    at_first, at_second = pl.ds(0, states), pl.ds(states, states)
    pl.when((p > 0) & first)(lambda: back(at_first, 0).start())
    pl.when((p > 0) & second)(lambda: back(at_second, 1).start())
    pl.when((p > 0) & first)(lambda: back_coef().start())
    pl.when(first)(lambda: to_second().start())
    pl.when(second)(lambda: to_first().start())

    @pl.when(first)
    def _():
        whole[0:states, :] = scaled[:, : mine + RIM]
        wide_ref[...] = coef_ref[:, : mine + RIM]
        to_first().wait_recv()

    @pl.when(second)
    def _():
        whole[states:, :mine] = scaled[:, mine:]
        wide_ref[:, :mine] = coef_ref[:, mine:]
        to_second().wait_recv()

    @pl.loop(0, mine // 128)
    def _(b):
        at = pl.ds(pl.multiple_of(b * 128, 128), 128)
        one_ref[at, :] = whole[:, at].T

    @pl.when(first)
    def _():
        @pl.loop(mine // 128, (mine + RIM) // 128)
        def _(b):
            at = pl.ds(pl.multiple_of(b * 128, 128), 128)
            one_ref[at, :] = whole[:, at].T

    @pl.when(second & (p == parts - 1))
    def _():
        tail[...] = jnp.zeros_like(tail)
        wide_ref[:, mine:] = jnp.zeros((wide_ref.shape[0], RIM), jnp.float32)

    @pl.when(second & (p < parts - 1))
    def _():
        back(at_first, 0).wait_recv()
        back(at_second, 1).wait_recv()
        back_coef().wait_recv()

    @pl.when(second)
    def _():
        @pl.loop(0, RIM // 128)
        def _(b):
            at = pl.multiple_of(b * 128, 128)
            one_ref[pl.ds(mine + at, 128), :] = tail[:, pl.ds(at, 128)].T

    pl.when((p > 0) & first)(lambda: back(at_first, 0).wait_send())
    pl.when((p > 0) & second)(lambda: back(at_second, 1).wait_send())
    pl.when((p > 0) & first)(lambda: back_coef().wait_send())
    pl.when(first)(lambda: to_second().wait_send())
    pl.when(second)(lambda: to_first().wait_send())


def spread(parts, columns, block, coef):
    states, owned = block.shape
    mine = owned // 2
    vmem = pl.BlockSpec(memory_space=pltpu.VMEM)
    f32 = jnp.float32
    return pl.pallas_call(
        functools.partial(spread_kernel, parts, columns),
        out_shape=(
            jax.ShapeDtypeStruct((mine + RIM, 2 * states), f32),
            jax.ShapeDtypeStruct((coef.shape[0], mine + RIM), f32),
        ),
        in_specs=[vmem] * 2,
        out_specs=(vmem, vmem),
        scratch_shapes=[
            pltpu.VMEM((states, owned), f32),
            pltpu.VMEM((2 * states, mine + RIM), f32),
            pltpu.VMEM((2 * states, RIM), f32),
            pltpu.SemaphoreType.DMA((2, 5)),
        ],
        compiler_params=pltpu.CompilerParams(
            collective_id=1, has_side_effects=True, vmem_limit_bytes=44 * 1024 * 1024
        ),
    )(block, coef)


def middle_kernel(parts, columns, sums_ref, one_ref, coef_ref, two_ref, lower, upper, sems):
    p, g, y, k = seat(columns)
    t, last = 2 * p + k, 2 * parts - 1
    mine = sums_ref.shape[0] - RIM

    def device(t):
        return (t // 2, 2 * y + lax.rem(t, 2))

    barrier = pltpu.get_barrier_semaphore()
    has_up, has_down = t < last, t > 0
    for have, to in ((has_up, t + 1), (has_down, t - 1)):
        pl.when(have)(
            lambda to=to: pl.semaphore_signal(
                barrier, inc=1, device_id=device(to), device_id_type=MESH
            )
        )
    pl.semaphore_wait(barrier, jnp.where(has_up, 1, 0) + jnp.where(has_down, 1, 0))

    def rise():
        return remote(sums_ref.at[pl.ds(mine, RIM)], lower, sems, 0, device(t + 1))

    def fall():
        return remote(sums_ref.at[pl.ds(0, RIM)], upper, sems, 1, device(t - 1))

    pl.when(has_up)(lambda: rise().start())
    pl.when(has_down)(lambda: fall().start())

    @pl.when(t == 0)
    def _():
        lower[...] = jnp.zeros_like(lower)

    @pl.when(t == last)
    def _():
        upper[...] = jnp.zeros_like(upper)

    def combine(b, extra, base):
        rows = pl.ds(pl.multiple_of(b * 128, 128), 128)
        value = sums_ref[rows, :]
        if extra is not None:
            value = value + extra[pl.ds(pl.multiple_of((b - base) * 128, 128), 128), :]
        size = (128, 128)
        one = jnp.broadcast_to(coef_ref[1:2, rows], size).T
        two = jnp.broadcast_to(coef_ref[2:3, rows], size).T
        two_ref[rows, :] = one * value + two * one_ref[rows, :]

    pl.loop(RIM // 128, mine // 128)(lambda b: combine(b, None, 0))
    pl.when(has_down)(lambda: rise().wait_recv())
    pl.loop(0, RIM // 128)(lambda b: combine(b, lower, 0))
    pl.when(has_up)(lambda: fall().wait_recv())
    pl.loop(mine // 128, (mine + RIM) // 128)(lambda b: combine(b, upper, mine // 128))
    pl.when(has_up)(lambda: rise().wait_send())
    pl.when(has_down)(lambda: fall().wait_send())


def middle(parts, columns, sums, one, coef):
    vmem = pl.BlockSpec(memory_space=pltpu.VMEM)
    rim = pltpu.VMEM((RIM, sums.shape[1]), jnp.float32)
    return pl.pallas_call(
        functools.partial(middle_kernel, parts, columns),
        out_shape=jax.ShapeDtypeStruct(sums.shape, jnp.float32),
        in_specs=[vmem] * 3,
        out_specs=vmem,
        scratch_shapes=[rim, rim, pltpu.SemaphoreType.DMA((2, 2))],
        compiler_params=pltpu.CompilerParams(
            collective_id=2, has_side_effects=True, vmem_limit_bytes=44 * 1024 * 1024
        ),
    )(sums, one, coef)


def shards(block, inv_sqrt_mass, potential, elem_scale, connectivity, elem_matrix):
    lowest, cut, top = (-2.0, 4.0, 32.0)
    half = (top - cut) / 2.0
    centre = (top + cut) / 2.0
    sigma = half / (lowest - centre)
    sigma_two = 1.0 / (2.0 / sigma - sigma)
    alpha, beta, gamma = sigma / half, 2.0 * (sigma_two / half), sigma * sigma_two
    parts = lax.axis_size("nodes")
    columns = lax.axis_size("grid")
    states, owned = block.shape
    mine = owned // 2
    core = lax.axis_index("grid") % 2
    elements = connectivity.shape[0] // 2
    index = lax.dynamic_slice_in_dim(connectivity, core * elements, elements, 0) - core * mine
    scale = lax.dynamic_slice_in_dim(elem_scale, core * elements, elements, 0)
    pad = -elem_matrix.shape[0] % 128
    matrix = jnp.pad(elem_matrix, ((0, pad), (0, pad)))

    shift = potential - centre
    inverse = 1.0 / inv_sqrt_mass
    zero = jnp.zeros_like(shift)
    coef = jnp.stack(
        [
            inv_sqrt_mass,
            alpha * inv_sqrt_mass * inv_sqrt_mass,
            alpha * shift,
            beta * inv_sqrt_mass,
            beta * shift * inverse,
            -gamma * inverse,
            zero,
            zero,
        ]
    )
    one, coef = spread(parts, columns, block, coef)
    sums = element_sums(one, index, scale, matrix)
    two = middle(parts, columns, sums, one, coef)
    sums = element_sums(two, index, scale, matrix)
    return finish(parts, columns, states, owned, sums, one, two, coef)


def solution(mesh):
    placed = (P("grid", "nodes"), P("nodes"), P("nodes"), P("nodes"), P("nodes", None), P())
    return jax.shard_map(
        shards,
        mesh=mesh,
        in_specs=placed,
        out_specs=(P("grid", "nodes"), P(None, "grid")),
        check_vma=False,
    )
```

```python
import functools
import jax
import jax.numpy as jnp
from jax import lax
from jax.experimental import pallas as pl
from jax.experimental.pallas import tpu as pltpu
from jax.sharding import PartitionSpec as P

RIM = 2048
NB = 128
SB = 16
GROUP = 4
CHAINS = 8
BOTH = ("nodes", "grid")


def split(value):
    high = value.astype(jnp.bfloat16)
    return high, (value - high.astype(jnp.float32)).astype(jnp.bfloat16)


def dot(a, b):
    return jnp.dot(a, b, preferred_element_type=jnp.float32)


def operator_kernel(
    npe, base, index_ref, scale_ref, matrix_ref, all_ref, near_ref, far_ref, picked, local, *sums
):
    wide_ref = all_ref.at[pl.ds(base, 2 * RIM)]
    groups = scale_ref.shape[0] // GROUP
    m_high, m_low = split(matrix_ref[...])
    picked[...] = jnp.zeros_like(picked)
    for total in sums:
        total[...] = jnp.zeros_like(total)

    def gather(first, i, m):
        node = index_ref[(first + m) * npe + i]
        picked[i : i + 1, m * 128 : (m + 1) * 128] = wide_ref[pl.ds(node, 1), :]

    for i in range(npe):
        for m in range(GROUP):
            gather(0, i, m)

    @pl.loop(0, groups)
    def _(g):
        here = g * GROUP
        later = jnp.minimum(g + 1, groups - 1) * GROUP
        high, low = split(picked[...])
        product = dot(m_high, high) + (dot(m_high, low) + dot(m_low, high))
        for m in range(GROUP):
            local[:, m * 128 : (m + 1) * 128] = (
                product[:, m * 128 : (m + 1) * 128] * scale_ref[here + m]
            )
        for i in range(npe):
            for m in range(GROUP):
                total = sums[(i * GROUP + m) % len(sums)]
                node = index_ref[(here + m) * npe + i]
                total[pl.ds(node, 1), :] += local[i : i + 1, m * 128 : (m + 1) * 128]
                gather(later, i, m)

    for target, start in ((near_ref, 0), (far_ref, RIM)):
        value = sums[0][start : start + RIM, :]
        for total in sums[1:]:
            value = value + total[start : start + RIM, :]
        target[...] = value


def element_sums(wide, base, index, scale, matrix):
    count, npe = index.shape
    piece = jax.ShapeDtypeStruct((RIM, wide.shape[1]), jnp.float32)
    vmem = pl.BlockSpec(memory_space=pltpu.VMEM)
    smem = pl.BlockSpec(memory_space=pltpu.SMEM)
    rows = matrix.shape[0]
    return pl.pallas_call(
        functools.partial(operator_kernel, npe, base),
        out_shape=(piece, piece),
        in_specs=[smem, smem, vmem, vmem],
        out_specs=(vmem, vmem),
        scratch_shapes=[pltpu.VMEM((rows, GROUP * 128), jnp.float32)] * 2
        + [pltpu.VMEM((2 * RIM, wide.shape[1]), jnp.float32)] * CHAINS,
        compiler_params=pltpu.CompilerParams(vmem_limit_bytes=44 * 1024 * 1024),
        cost_estimate=pl.CostEstimate(
            flops=6 * count * rows * rows * wide.shape[1],
            bytes_accessed=4 * (wide.size + 2 * piece.size + 8 * count * npe * wide.shape[1]),
            transcendentals=0,
        ),
    )((index - base).reshape(-1), scale, matrix, wide)


def both_sums(wide, index, scale, matrix, ups):
    half = index.shape[0] // 2
    inner, rim = element_sums(wide, RIM, index[half:], scale[half:], matrix)
    lower = lax.ppermute(rim, BOTH, ups)
    wide, rim = lax.optimization_barrier((wide, rim))
    near, far = element_sums(wide, 0, index[:half], scale[:half], matrix)
    return near, far, inner, rim, lower


STRIDE = 11
MESH = pl.DeviceIdType.MESH


def others(count, me, body, begin=1, end=None):
    stride = STRIDE if count % STRIDE else 1

    def step(s, carry):
        body(lax.rem(me + s * stride, count))
        return carry

    lax.fori_loop(begin, end or count, step, 0)


def finish_kernel(
    parts, columns, pieces, weight,
    near_ref, far_ref, inner_ref, lower_ref, one_ref, two_ref, coef_ref, out_ref, panel_ref,
    flat, send, raw, high, low, gram, collected, stage, panel,
    swap_sem, move_send, move_recv, part_send, part_recv, row_send, row_recv, own_sem,
):
    p, g = lax.axis_index("nodes"), lax.axis_index("grid")
    y, k = g // 2, lax.rem(g, 2)
    count = parts * columns
    me = p * columns + g
    mine = flat.shape[1]
    quarter = mine // 4
    width = mine // parts
    span = width // pieces
    states = panel_ref.shape[1]
    total_states = gram.shape[0]
    owners = total_states // 8

    def place(d):
        return (d // columns, lax.rem(d, columns))

    barrier = pltpu.get_barrier_semaphore()
    others(
        count, me,
        lambda d: pl.semaphore_signal(barrier, inc=1, device_id=place(d), device_id_type=MESH),
    )
    pl.semaphore_wait(barrier, count - 1)

    def swap_copy(h):
        start = pl.multiple_of((2 * h + 1 - y) * quarter, 128)
        return pltpu.make_async_remote_copy(
            src_ref=flat.at[:, pl.ds(start, quarter)],
            dst_ref=raw.at[h, pl.ds(pl.multiple_of(y * 128, 128), 128)],
            send_sem=swap_sem.at[0, h], recv_sem=swap_sem.at[1, h],
            device_id=(p, 2 * (1 - y) + k), device_id_type=MESH,
        )

    def landing(d, h):
        dp, dg = place(d)
        row = pl.multiple_of((dg // 2) * 32, 32)
        column = pl.multiple_of((dp * 2 + lax.rem(dg, 2)) * width + h * span, 128)
        return out_ref.at[pl.ds(row, 32), pl.ds(column, span)]

    def move(d, h, source):
        return pltpu.make_async_remote_copy(
            src_ref=send.at[d, :, pl.ds(h * span, span)], dst_ref=landing(source, h),
            send_sem=move_send.at[h, d], recv_sem=move_recv.at[h, source],
            device_id=place(d), device_id_type=MESH,
        )

    def combine(b, with_rim):
        at = pl.multiple_of(b * 128, 128)
        rows = pl.ds(at, 128)
        if with_rim:
            value = near_ref[rows, :] + lower_ref[rows, :]
        else:
            behind = pl.ds(pl.multiple_of(at - RIM, 128), 128)
            value = far_ref[behind, :] + inner_ref[behind, :]
        result = (
            value.T * coef_ref[3:4, rows]
            + two_ref[rows, :].T * coef_ref[4:5, rows]
            + one_ref[rows, :].T * coef_ref[5:6, rows]
        )
        flat[:, rows] = result
        l, q = b // parts, lax.rem(b, parts)
        for c in range(columns):
            for kk in range(2):
                send[q * columns + c, kk * SB : (kk + 1) * SB, pl.ds(pl.multiple_of(l * 128, 128), 128)] = (
                    result[kk * states + c * SB : kk * states + (c + 1) * SB, :]
                )

    half = mine // 256

    def keep(h):
        start = pl.multiple_of((2 * h + y) * quarter, 128)
        raw[h, pl.ds(pl.multiple_of(y * 128, 128), 128), :] = flat[:, pl.ds(start, quarter)]

    @pl.loop(half, 2 * half)
    def _(b):
        combine(b, False)

    swap_copy(1).start()
    if pieces == 2:
        others(count, me, lambda d: move(d, 1, me).start())
    keep(1)

    @pl.loop(0, half)
    def _(b):
        combine(b, True)

    swap_copy(0).start()
    others(count, me, lambda d: move(d, 0, me).start(), 1, count // 2)
    keep(0)
    own = [
        pltpu.make_async_copy(send.at[me, :, pl.ds(h * span, span)], landing(me, h), own_sem.at[h])
        for h in range(pieces)
    ]
    for copy in own:
        copy.start()

    across = (((1,), (1,)), ((), ()))

    def product(a, b):
        return lax.dot_general(a, b, across, preferred_element_type=jnp.float32)

    for h in (1, 0):
        swap_copy(h).wait_recv()
        for c in range(columns):
            for kb in range(columns):
                upper, lower = split(raw[h, kb * states + c * SB : kb * states + (c + 1) * SB, :])
                to = c * states + kb * SB
                high[to : to + SB, :] = upper
                low[to : to + SB, :] = lower
        mixed = product(high[...], low[...])
        value = product(high[...], high[...]) + (mixed + mixed.T)
        if h == 1:
            gram[...] = value
        else:
            gram[...] = gram[...] + value

    def rows_of(d):
        return pl.ds(pl.multiple_of(d * 8, 8), 8)

    def part(d, source):
        return pltpu.make_async_remote_copy(
            src_ref=gram.at[rows_of(d)], dst_ref=collected.at[source],
            send_sem=part_send.at[d], recv_sem=part_recv.at[source],
            device_id=place(d), device_id_type=MESH,
        )

    def if_owner(d, body):
        if owners == count:
            body()
        else:
            pl.when(d < owners)(body)

    def row(d, source):
        return pltpu.make_async_remote_copy(
            src_ref=stage.at[lax.rem(d, columns)], dst_ref=panel.at[rows_of(source)],
            send_sem=row_send.at[d], recv_sem=row_recv.at[source],
            device_id=place(d), device_id_type=MESH,
        )

    others(count, me, lambda d: if_owner(d, lambda: part(d, me).start()))
    others(count, me, lambda d: move(d, 0, me).start(), count // 2, count)
    stage[...] = jnp.zeros_like(stage)

    def own_rows():
        collected[me] = gram[rows_of(me), :]
        others(count, me, lambda d: part(me, d).wait_recv())
        sums = lax.fori_loop(
            0, count, lambda d, value: value + collected[d], jnp.zeros(collected.shape[1:], jnp.float32)
        )
        sums = sums * weight
        for c in range(columns):
            stage[c, :, :states] = sums[:, c * states : (c + 1) * states]
        panel[rows_of(me), :] = stage[g]
        others(count, me, lambda d: row(d, me).start())

    if_owner(me, own_rows)
    others(count, me, lambda d: if_owner(d, lambda: row(me, d).wait_recv()))
    panel_ref[...] = panel[:, :states]

    for h in range(pieces):
        others(count, me, lambda d: move(me, h, d).wait_recv())
    for h in range(pieces):
        others(count, me, lambda d: move(d, h, me).wait_send())
    for copy in own:
        copy.wait()
    for h in (0, 1):
        swap_copy(h).wait_send()
    others(count, me, lambda d: if_owner(d, lambda: part(d, me).wait_send()))
    if_owner(me, lambda: others(count, me, lambda d: row(d, me).wait_send()))


def finish(parts, columns, states, owned, near, far, inner, lower, one, two, coef):
    mine = owned // 2
    count = parts * columns
    width = mine // parts
    pieces = 2 if width % 256 == 0 else 1
    total = columns * states
    vmem = pl.BlockSpec(memory_space=pltpu.VMEM)
    dma = pltpu.SemaphoreType.DMA
    f32, bf16 = jnp.float32, jnp.bfloat16
    return pl.pallas_call(
        functools.partial(finish_kernel, parts, columns, pieces, 1.0 / (owned * parts)),
        out_shape=(
            jax.ShapeDtypeStruct((states, owned), f32),
            jax.ShapeDtypeStruct((total, states), f32),
        ),
        in_specs=[vmem] * 7,
        out_specs=(pl.BlockSpec(memory_space=pl.ANY), vmem),
        scratch_shapes=[
            pltpu.VMEM((2 * states, mine), f32),
            pltpu.VMEM((count, 2 * SB, width), f32),
            pltpu.VMEM((2, total, mine // 4), f32),
            pltpu.VMEM((total, mine // 4), bf16),
            pltpu.VMEM((total, mine // 4), bf16),
            pltpu.VMEM((total, total), f32),
            pltpu.VMEM((count, 8, total), f32),
            pltpu.VMEM((columns, 8, 128), f32),
            pltpu.VMEM((total, 128), f32),
            dma((2, 2)), dma((pieces, count)), dma((pieces, count)),
            dma((count,)), dma((count,)), dma((count,)), dma((count,)), dma((pieces,)),
        ],
        compiler_params=pltpu.CompilerParams(
            collective_id=0, has_side_effects=True, vmem_limit_bytes=44 * 1024 * 1024
        ),
    )(near, far, inner, lower, one, two, coef)


def seat(columns):
    p, g = lax.axis_index("nodes"), lax.axis_index("grid")
    return p, g, g // 2, lax.rem(g, 2)


def remote(source, target, sems, slot, device):
    return pltpu.make_async_remote_copy(
        src_ref=source, dst_ref=target, send_sem=sems.at[0, slot], recv_sem=sems.at[1, slot],
        device_id=device, device_id_type=MESH,
    )


def spread_kernel(
    parts, columns, block_ref, coef_ref, one_ref, wide_ref, scaled, whole, tail, sems
):
    p, g, y, k = seat(columns)
    states, owned = block_ref.shape
    mine = owned // 2
    barrier = pltpu.get_barrier_semaphore()
    pl.semaphore_signal(barrier, inc=1, device_id=(p, 2 * y + 1 - k), device_id_type=MESH)

    @pl.when(p > 0)
    def _():
        pl.semaphore_signal(barrier, inc=1, device_id=(p - 1, 2 * y + 1), device_id_type=MESH)

    @pl.when((k == 1) & (p < parts - 1))
    def _():
        for kk in range(2):
            pl.semaphore_signal(barrier, inc=1, device_id=(p + 1, 2 * y + kk), device_id_type=MESH)

    rows = pl.ds(pl.multiple_of(k * states, 8), states)

    @pl.loop(0, owned // 512)
    def _(b):
        at = pl.ds(pl.multiple_of(b * 512, 128), 512)
        scaled[:, at] = block_ref[:, at] * coef_ref[0:1, at]

    before = jnp.where(p > 0, 1, 0)
    after = jnp.where((k == 1) & (p < parts - 1), 2, 0)
    pl.semaphore_wait(barrier, 1 + before + after)

    def back(r=rows, slot=0):
        return remote(scaled.at[:, pl.ds(0, RIM)], tail.at[r], sems, slot, (p - 1, 2 * y + 1))

    def back_coef():
        return remote(
            coef_ref.at[:, pl.ds(0, RIM)], wide_ref.at[:, pl.ds(mine, RIM)], sems, 2,
            (p - 1, 2 * y + 1),
        )

    def to_second():
        return remote(
            scaled.at[:, pl.ds(mine, mine)], whole.at[rows, pl.ds(0, mine)], sems, 3,
            (p, 2 * y + 1),
        )

    def to_first():
        return remote(
            scaled.at[:, pl.ds(0, mine + RIM)], whole.at[rows], sems, 4, (p, 2 * y)
        )

    first, second = k == 0, k == 1
    at_first, at_second = pl.ds(0, states), pl.ds(states, states)
    pl.when((p > 0) & first)(lambda: back(at_first, 0).start())
    pl.when((p > 0) & second)(lambda: back(at_second, 1).start())
    pl.when((p > 0) & first)(lambda: back_coef().start())
    pl.when(first)(lambda: to_second().start())
    pl.when(second)(lambda: to_first().start())

    @pl.when(first)
    def _():
        whole[0:states, :] = scaled[:, : mine + RIM]
        wide_ref[...] = coef_ref[:, : mine + RIM]
        to_first().wait_recv()

    @pl.when(second)
    def _():
        whole[states:, :mine] = scaled[:, mine:]
        wide_ref[:, :mine] = coef_ref[:, mine:]
        to_second().wait_recv()

    @pl.loop(0, mine // 128)
    def _(b):
        at = pl.ds(pl.multiple_of(b * 128, 128), 128)
        one_ref[at, :] = whole[:, at].T

    @pl.when(first)
    def _():
        @pl.loop(mine // 128, (mine + RIM) // 128)
        def _(b):
            at = pl.ds(pl.multiple_of(b * 128, 128), 128)
            one_ref[at, :] = whole[:, at].T

    @pl.when(second & (p == parts - 1))
    def _():
        tail[...] = jnp.zeros_like(tail)
        wide_ref[:, mine:] = jnp.zeros((wide_ref.shape[0], RIM), jnp.float32)

    @pl.when(second & (p < parts - 1))
    def _():
        back(at_first, 0).wait_recv()
        back(at_second, 1).wait_recv()
        back_coef().wait_recv()

    @pl.when(second)
    def _():
        @pl.loop(0, RIM // 128)
        def _(b):
            at = pl.multiple_of(b * 128, 128)
            one_ref[pl.ds(mine + at, 128), :] = tail[:, pl.ds(at, 128)].T

    pl.when((p > 0) & first)(lambda: back(at_first, 0).wait_send())
    pl.when((p > 0) & second)(lambda: back(at_second, 1).wait_send())
    pl.when((p > 0) & first)(lambda: back_coef().wait_send())
    pl.when(first)(lambda: to_second().wait_send())
    pl.when(second)(lambda: to_first().wait_send())


def spread(parts, columns, block, coef):
    states, owned = block.shape
    mine = owned // 2
    vmem = pl.BlockSpec(memory_space=pltpu.VMEM)
    f32 = jnp.float32
    return pl.pallas_call(
        functools.partial(spread_kernel, parts, columns),
        out_shape=(
            jax.ShapeDtypeStruct((mine + RIM, 2 * states), f32),
            jax.ShapeDtypeStruct((coef.shape[0], mine + RIM), f32),
        ),
        in_specs=[vmem] * 2,
        out_specs=(vmem, vmem),
        scratch_shapes=[
            pltpu.VMEM((states, owned), f32),
            pltpu.VMEM((2 * states, mine + RIM), f32),
            pltpu.VMEM((2 * states, RIM), f32),
            pltpu.SemaphoreType.DMA((2, 5)),
        ],
        compiler_params=pltpu.CompilerParams(
            collective_id=1, has_side_effects=True, vmem_limit_bytes=44 * 1024 * 1024
        ),
    )(block, coef)


def middle_kernel(
    parts, columns, near_ref, far_ref, inner_ref, rim_ref, lower_ref, one_ref, coef_ref, two_ref, upper, sems
):
    p, g, y, k = seat(columns)
    t, last = 2 * p + k, 2 * parts - 1

    def device(t):
        return (t // 2, 2 * y + lax.rem(t, 2))

    barrier = pltpu.get_barrier_semaphore()
    has_up, has_down = t < last, t > 0
    for have, to in ((has_up, t + 1), (has_down, t - 1)):
        pl.when(have)(
            lambda to=to: pl.semaphore_signal(
                barrier, inc=1, device_id=device(to), device_id_type=MESH
            )
        )
    pl.semaphore_wait(barrier, jnp.where(has_up, 1, 0) + jnp.where(has_down, 1, 0))

    def fall():
        return remote(near_ref, upper, sems, 0, device(t - 1))

    pl.when(has_down)(lambda: fall().start())

    @pl.when(t == last)
    def _():
        upper[...] = jnp.zeros_like(upper)

    def combine(base, a_ref, b_ref):
        @pl.loop(0, RIM // 128)
        def _(b):
            here = pl.ds(pl.multiple_of(b * 128, 128), 128)
            rows = pl.ds(pl.multiple_of(base + b * 128, 128), 128)
            size = (128, 128)
            one = jnp.broadcast_to(coef_ref[1:2, rows], size).T
            two = jnp.broadcast_to(coef_ref[2:3, rows], size).T
            value = a_ref[here, :] + b_ref[here, :]
            two_ref[rows, :] = one * value + two * one_ref[rows, :]

    combine(0, near_ref, lower_ref)
    combine(RIM, far_ref, inner_ref)
    pl.when(has_up)(lambda: fall().wait_recv())
    combine(2 * RIM, rim_ref, upper)
    pl.when(has_down)(lambda: fall().wait_send())


def middle(parts, columns, near, far, inner, rim, lower, one, coef):
    vmem = pl.BlockSpec(memory_space=pltpu.VMEM)
    return pl.pallas_call(
        functools.partial(middle_kernel, parts, columns),
        out_shape=jax.ShapeDtypeStruct(one.shape, jnp.float32),
        in_specs=[vmem] * 7,
        out_specs=vmem,
        scratch_shapes=[pltpu.VMEM(near.shape, jnp.float32), pltpu.SemaphoreType.DMA((2, 1))],
        compiler_params=pltpu.CompilerParams(
            collective_id=2, has_side_effects=True, vmem_limit_bytes=44 * 1024 * 1024
        ),
    )(near, far, inner, rim, lower, one, coef)


def shards(block, inv_sqrt_mass, potential, elem_scale, connectivity, elem_matrix):
    lowest, cut, top = (-2.0, 4.0, 32.0)
    half = (top - cut) / 2.0
    centre = (top + cut) / 2.0
    sigma = half / (lowest - centre)
    sigma_two = 1.0 / (2.0 / sigma - sigma)
    alpha, beta, gamma = sigma / half, 2.0 * (sigma_two / half), sigma * sigma_two
    parts = lax.axis_size("nodes")
    columns = lax.axis_size("grid")
    states, owned = block.shape
    mine = owned // 2
    core = lax.axis_index("grid") % 2
    elements = connectivity.shape[0] // 2
    index = lax.dynamic_slice_in_dim(connectivity, core * elements, elements, 0) - core * mine
    scale = lax.dynamic_slice_in_dim(elem_scale, core * elements, elements, 0)
    pad = -elem_matrix.shape[0] % 128
    matrix = jnp.pad(elem_matrix, ((0, pad), (0, pad)))

    shift = potential - centre
    inverse = 1.0 / inv_sqrt_mass
    zero = jnp.zeros_like(shift)
    coef = jnp.stack(
        [
            inv_sqrt_mass,
            alpha * inv_sqrt_mass * inv_sqrt_mass,
            alpha * shift,
            beta * inv_sqrt_mass,
            beta * shift * inverse,
            -gamma * inverse,
            zero,
            zero,
        ]
    )
    one, coef = spread(parts, columns, block, coef)
    ups = []
    for y in range(columns // 2):
        for t in range(2 * parts - 1):
            below = (t // 2) * columns + 2 * y + t % 2
            ups.append((below, ((t + 1) // 2) * columns + 2 * y + (t + 1) % 2))
    near, far, inner, rim, lower = both_sums(one, index, scale, matrix, ups)
    two = middle(parts, columns, near, far, inner, rim, lower, one, coef)
    near, far, inner, rim, lower = both_sums(two, index, scale, matrix, ups)
    return finish(parts, columns, states, owned, near, far, inner, lower, one, two, coef)


def solution(mesh):
    placed = (P("grid", "nodes"), P("nodes"), P("nodes"), P("nodes"), P("nodes", None), P())
    return jax.shard_map(
        shards,
        mesh=mesh,
        in_specs=placed,
        out_specs=(P("grid", "nodes"), P(None, "grid")),
        check_vma=False,
    )
```
